32 devices in a mesh: group: 2 (over y), row: 4 (over z), blk: 2 (over x), span: 2 (over core).
Axes of the slice: x: 2, y: 2, z: 4, core: 2. Of those that a mesh axis runs over, the one named last changes fastest.
Arguments:
- adjoint_in: bfloat16 [1024, 10, 32, 256], P('row', 'group', 'blk', 'span'), parts along dimension 1, may hold values from -6 to 6
- stencil_coef: float32 [10, 32, 256], P('group', 'blk', 'span'), parts along dimension 0, may hold values from -0.6 to 0.6
- rotor_lag: float32 [32], P('group'), parts along dimension 0, may hold values from -3.140625 to 3.140625
- stator_lag: float32 [24], P('group'), parts along dimension 0, may hold values from -3.140625 to 3.140625
- rotor_harm: int32 [256], replicated, may hold values from 0 to 15
- stator_harm: int32 [256], replicated, may hold values from 0 to 11
Outputs:
- adjoint_out: bfloat16 [1024, 10, 32, 256], P('row', 'group', 'blk', 'span'), parts along dimension 1
The draws below stay inside these ranges and needn't reach their ends.
There are 2 independent parts, one for each index of `group`. The reference program is written for one: setup_inputs(seed, part) draws one part's arguments, and reference() takes and returns one part's arrays. A program takes and returns all parts, laid end to end along the dimension named above; an argument that names none is the same for every part. Nothing has to cross between parts.
All inputs are finite; a program needn't handle non-finite values.
Results may differ from the reference program's by a relative error of at most 0.0058.
Values may be sent and summed in bfloat16 or wider, within the bound.
A program may use at most 192 MiB of HBM per device.

```python
import math
import jax
import jax.numpy as jnp
from jax import lax

AZ = 1024
MODES = 256
HROT = 16
HSTA = 12
STATES = 5
SUBIT = 1
NX = 32
NS = 256


def set_ends(result, rng, smallest, top_value):
    shape = result.shape
    place = [jax.random.randint(jax.random.fold_in(rng, axis), (), 0, shape[axis]) for axis in range(len(shape))]
    result = result.at[tuple(place)].set(smallest)
    longest = shape.index(max(shape))
    place[longest] = (place[longest] + 1) % shape[longest]
    return result.at[tuple(place)].set(top_value)


def steps_of(rng, shape, cuts, least, largest):
    factor_of = 1.0
    for dim, blocks in cuts:
        steps = jax.random.uniform(jax.random.fold_in(jax.random.fold_in(rng, 6), dim), (blocks,), jnp.float32, least / len(cuts), largest / len(cuts))
        factor_of = factor_of * jnp.repeat(jnp.exp(steps), shape[dim] // blocks).reshape((-1,) + (1,) * (len(shape) - 1 - dim))
    return factor_of


def noise(rng, shape, spread, most, shards=(), kind=jnp.bfloat16):
    values = jax.random.normal(rng, shape, jnp.float32) * spread
    if len(shards) > 0:
        values = steps_of(rng, shape, shards, -0.22, 0.18) * values
    return jnp.clip(values, min=-most, max=most).astype(kind)


def setup_inputs(seed: int = 0, part: int = 0) -> dict:
    key_of = jax.random.split(jax.random.key(seed), 7)
    own_keys = jax.random.split(jax.random.fold_in(key_of[6], part), 7)
    return {
        "adjoint_in": noise(own_keys[0], (AZ, STATES, NX, NS), 1.0, 6.0, ((0, 4), (2, 2), (3, 2))),
        "stencil_coef": jnp.clip(jax.random.uniform(own_keys[1], (5, NX, NS), jnp.float32, -0.6, 0.6) * steps_of(own_keys[1], (5, NX, NS), ((1, 2), (2, 2)), -0.4, 0.0), -0.6, 0.6),
        "rotor_lag": jnp.clip(jax.random.uniform(own_keys[2], (HROT,), jnp.float32, -3.140625, 3.140625), -3.140625, 3.140625),
        "stator_lag": jnp.clip(jax.random.uniform(own_keys[3], (HSTA,), jnp.float32, -3.140625, 3.140625), -3.140625, 3.140625),
        "rotor_harm": set_ends(jax.random.randint(key_of[4], (MODES,), 0, HROT), jax.random.fold_in(key_of[4], 1), 0, HROT - 1).astype(jnp.int32),
        "stator_harm": set_ends(jax.random.randint(key_of[5], (MODES,), 0, HSTA), jax.random.fold_in(key_of[5], 1), 0, HSTA - 1).astype(jnp.int32),
    }


def make_table(points, modes_count):
    point_idx = jnp.arange(points, dtype=jnp.int32)
    mode_order = jnp.arange(1, modes_count + 1, dtype=jnp.int32)
    phase_idx = (point_idx[:, None] * mode_order[None, :]) % points
    angles = phase_idx.astype(jnp.float32) * (2.0 * math.pi / points)
    return jnp.concatenate([jnp.cos(angles), jnp.sin(angles)], axis=1).astype(jnp.bfloat16)


def reference(adjoint_in, stencil_coef, rotor_lag, stator_lag, rotor_harm, stator_harm):
    mode_table = make_table(AZ, MODES)
    axial_pos = jnp.arange(NX, dtype=jnp.int32)
    in_rotor = (axial_pos < NX // 2)[None, :]
    phase_angle = jnp.where(in_rotor, rotor_lag[rotor_harm][:, None], stator_lag[stator_harm][:, None])
    cos_scale = jnp.cos(phase_angle)[:, :, None]
    sin_scale = jnp.sin(phase_angle)[:, :, None]

    def one_state(state_field):
        values = state_field.astype(jnp.float32)
        summed = stencil_coef[0] * values
        summed = summed + jnp.pad((stencil_coef[1] * values)[:, 1:, :], ((0, 0), (0, 1), (0, 0)))
        summed = summed + jnp.pad((stencil_coef[2] * values)[:, :-1, :], ((0, 0), (1, 0), (0, 0)))
        summed = summed + jnp.pad((stencil_coef[3] * values)[:, :, 1:], ((0, 0), (0, 0), (0, 1)))
        summed = summed + jnp.pad((stencil_coef[4] * values)[:, :, :-1], ((0, 0), (0, 0), (1, 0)))
        coeffs = lax.dot_general(mode_table, state_field.reshape(AZ, -1), (((0,), (0,)), ((), ())),
                                 preferred_element_type=jnp.float32)
        coeffs = coeffs.reshape(2 * MODES, NX, NS)
        cos_part = coeffs[:MODES]
        sin_part = coeffs[MODES:]
        rotated = jnp.concatenate([cos_scale * cos_part + sin_scale * sin_part,
                                   cos_scale * sin_part - sin_scale * cos_part], axis=0).astype(jnp.bfloat16)
        synthesis = jnp.dot(mode_table, rotated.reshape(2 * MODES, -1), preferred_element_type=jnp.float32)
        synthesis = (synthesis * (2.0 / AZ)).reshape(AZ, NX, NS).astype(jnp.bfloat16)
        return (summed + synthesis.astype(jnp.float32)).astype(jnp.bfloat16)

    adjoint_field = jnp.moveaxis(adjoint_in, 1, 0)
    for sub_step in range(SUBIT):
        adjoint_field = lax.map(one_state, adjoint_field)
    return jnp.moveaxis(adjoint_field, 0, 1)
```

```python
import functools
import math

import jax
import jax.numpy as jnp
import numpy as np
from jax import lax
from jax.experimental import pallas as pl
from jax.experimental.pallas import tpu as pltpu
from jax.sharding import PartitionSpec as P

AZ = 1024
MODES = 256
LANES = 128
MESH = pl.DeviceIdType.MESH


def make_table(points, modes_count):
    point_idx = np.arange(points, dtype=np.int64)
    mode_order = np.arange(1, modes_count + 1, dtype=np.int64)
    phase_idx = point_idx[:, None] * mode_order[None, :] % points
    angles = phase_idx.astype(np.float32) * np.float32(2.0 * math.pi / points)
    return np.concatenate([np.cos(angles), np.sin(angles)], axis=1).astype(jnp.bfloat16)


def table_lookup(index_arr, lag_table):
    matches = index_arr[:, None] == jnp.arange(lag_table.shape[0], dtype=jnp.int32)[None, :]
    return jnp.sum(jnp.where(matches, lag_table[None, :], 0.0), axis=1)


def lanes_at(start, size):
    return pl.ds(pl.multiple_of(start, LANES), size)


def kernel(
    states, x_dev, chunk,
    f_ref, coef_ref, scale_ref, analysis_ref, table_ref,
    out_ref,
    gath, stage, ret, local, across, first_x, last_x, coef_got,
    fwd_send, fwd_recv, back_send, back_recv, halo_send, halo_recv,
):
    n = lax.axis_size("row")
    me = lax.axis_index("row")
    blks = lax.axis_size("blk")
    blk = lax.axis_index("blk")
    span = lax.axis_index("span")
    rows, columns = f_ref.shape
    share = columns // n
    chunks = share // chunk
    modes = table_ref.shape[1] // 2
    plane = x_dev * LANES

    peers = [lax.rem(me + off, n) for off in range(1, n)]
    sources = [lax.rem(me + n - off, n) for off in range(1, n)]
    blk_next = lax.rem(blk + 1, blks)
    blk_prev = lax.rem(blk + blks - 1, blks)
    span_other = 1 - span

    barrier = pltpu.get_barrier_semaphore()
    for peer in peers:
        pl.semaphore_signal(barrier, inc=1, device_id={"row": peer}, device_id_type=MESH)
    pl.semaphore_signal(barrier, inc=1, device_id={"blk": blk_next}, device_id_type=MESH)
    pl.semaphore_signal(barrier, inc=1, device_id={"blk": blk_prev}, device_id_type=MESH)
    pl.semaphore_signal(barrier, inc=1, device_id={"span": span_other}, device_id_type=MESH)
    pl.semaphore_wait(barrier, n + 2)

    def forward(ch, off, peer):
        return pltpu.make_async_remote_copy(
            src_ref=f_ref.at[:, lanes_at(peer * share + ch * chunk, chunk)],
            dst_ref=gath.at[pl.ds(pl.multiple_of(me * rows, 16), rows), lanes_at(ch * chunk, chunk)],
            send_sem=fwd_send.at[ch, off],
            recv_sem=fwd_recv.at[ch, off],
            device_id={"row": peer},
            device_id_type=MESH,
        )

    def backward(ch, off, peer):
        return pltpu.make_async_remote_copy(
            src_ref=stage.at[pl.ds(pl.multiple_of(peer * rows, 16), rows), lanes_at(ch * chunk, chunk)],
            dst_ref=ret.at[:, lanes_at(me * share + ch * chunk, chunk)],
            send_sem=back_send.at[ch, off],
            recv_sem=back_recv.at[ch, off],
            device_id={"row": peer},
            device_id_type=MESH,
        )

    def halo(idx, src, dst, where):
        return pltpu.make_async_remote_copy(
            src_ref=src, dst_ref=dst,
            send_sem=halo_send.at[idx], recv_sem=halo_recv.at[idx],
            device_id=where, device_id_type=MESH,
        )

    halos = [
        halo(0, coef_ref, coef_got.at[0], {"span": span_other}),
        halo(1, coef_ref, coef_got.at[1], {"blk": blk_prev}),
        halo(2, coef_ref, coef_got.at[2], {"blk": blk_next}),
        halo(3, f_ref, across, {"span": span_other}),
    ]
    for c in range(states):
        here = pl.ds(c * LANES, LANES)
        halos.append(halo(4 + 2 * c, f_ref.at[:, pl.ds(c * plane, LANES)], first_x.at[:, here], {"blk": blk_prev}))
        halos.append(
            halo(5 + 2 * c, f_ref.at[:, pl.ds((c + 1) * plane - LANES, LANES)], last_x.at[:, here], {"blk": blk_next})
        )

    @pl.loop(0, chunks)
    def _(ch):
        for off, peer in enumerate(peers):
            forward(ch, off, peer).start()

    for copy in halos:
        copy.start()

    gath[pl.ds(pl.multiple_of(me * rows, 16), rows), :] = f_ref[:, lanes_at(me * share, share)]

    cos_scale = scale_ref[:, 0:1]
    sin_scale = scale_ref[:, 1:2]

    @pl.loop(0, chunks)
    def _(ch):
        for off, peer in enumerate(peers):
            forward(ch, off, peer).wait_recv()
        here = lanes_at(ch * chunk, chunk)
        coeffs = jnp.dot(analysis_ref[...], gath[:, here], preferred_element_type=jnp.float32)
        cos_part = coeffs[:modes]
        sin_part = coeffs[modes:]
        rotated = jnp.concatenate(
            [cos_scale * cos_part + sin_scale * sin_part, cos_scale * sin_part - sin_scale * cos_part], axis=0
        ).astype(jnp.bfloat16)
        synthesis = jnp.dot(table_ref[...], rotated, preferred_element_type=jnp.float32)
        stage[:, here] = (synthesis * (2.0 / AZ)).astype(jnp.bfloat16)
        for off, peer in enumerate(peers):
            backward(ch, off, peer).start()
        ret[:, lanes_at(me * share + ch * chunk, chunk)] = stage[pl.ds(pl.multiple_of(me * rows, 16), rows), here]

    for copy in halos:
        copy.wait_recv()

    step = 64
    lane = lax.broadcasted_iota(jnp.int32, (step, LANES), 1)
    has_next = blk < blks - 1
    has_prev = blk > 0

    @pl.loop(0, states)
    def _(c):
        @pl.loop(0, rows // step)
        def _(rb):
            here = pl.ds(pl.multiple_of(rb * step, step), step)

            def field_at(x):
                return f_ref[here, lanes_at(c * plane + x * LANES, LANES)].astype(jnp.float32)

            def other_at(x):
                return across[here, lanes_at(c * plane + x * LANES, LANES)].astype(jnp.float32)

            def coef_at(k, x):
                return coef_ref[k : k + 1, x * LANES : (x + 1) * LANES]

            edge = lanes_at(c * LANES, LANES)
            before = coef_got[2, 2:3, plane - LANES : plane] * last_x[here, edge].astype(jnp.float32)
            after = coef_got[1, 1:2, 0:LANES] * first_x[here, edge].astype(jnp.float32)
            before = jnp.where(has_prev, before, 0.0)
            after = jnp.where(has_next, after, 0.0)
            now = field_at(0)
            prev_term = before
            for x in range(x_dev):
                later = field_at(x + 1) if x + 1 < x_dev else None
                next_term = coef_at(1, x + 1) * later if later is not None else after
                other = other_at(x)
                cols = slice(x * LANES, (x + 1) * LANES)
                right_edge = jnp.where(span == 0, coef_got[0, 3:4, cols] * other, 0.0)
                left_edge = jnp.where(span == 1, coef_got[0, 4:5, cols] * other, 0.0)
                right = pltpu.roll(jnp.where(lane == 0, right_edge, coef_at(3, x) * now), LANES - 1, 1)
                left = pltpu.roll(jnp.where(lane == LANES - 1, left_edge, coef_at(4, x) * now), 1, 1)
                local[here, lanes_at(c * plane + x * LANES, LANES)] = (
                    coef_at(0, x) * now + next_term + prev_term + right + left
                )
                prev_term = coef_at(2, x) * now
                now = later

    def finish(start):
        cols = lanes_at(start, chunk)
        out_ref[:, cols] = (local[:, cols] + ret[:, cols].astype(jnp.float32)).astype(jnp.bfloat16)

    @pl.loop(0, chunks)
    def _(ch):
        finish(me * share + ch * chunk)

    @pl.loop(0, chunks)
    def _(ch):
        for off, (peer, source) in enumerate(zip(peers, sources)):
            backward(ch, off, peer).wait_recv()
            finish(source * share + ch * chunk)

    @pl.loop(0, chunks)
    def _(ch):
        for off, peer in enumerate(peers):
            forward(ch, off, peer).wait_send()
            backward(ch, off, peer).wait_send()

    for copy in halos:
        copy.wait_send()


def on_device(adjoint_in, stencil_coef, rotor_lag, stator_lag, rotor_harm, stator_harm):
    rows, states, x_dev, s_dev = adjoint_in.shape
    n = lax.axis_size("row")
    columns = states * x_dev * s_dev
    tiles = columns // n // LANES
    chunk = LANES * max(d for d in (1, 2, 4) if tiles % d == 0)
    chunks = columns // n // chunk
    table = make_table(AZ, MODES)
    in_rotor = lax.axis_index("blk") * 2 < lax.axis_size("blk")
    phase_angle = jnp.where(in_rotor, table_lookup(rotor_harm, rotor_lag), table_lookup(stator_harm, stator_lag))
    scale = jnp.stack([jnp.cos(phase_angle), jnp.sin(phase_angle)], axis=1)
    coef = jnp.pad(stencil_coef.reshape(5, x_dev * s_dev), ((0, 3), (0, 0)))
    vmem = pl.BlockSpec(memory_space=pltpu.VMEM)
    dma = pltpu.SemaphoreType.DMA
    out = pl.pallas_call(
        functools.partial(kernel, states, x_dev, chunk),
        out_shape=jax.ShapeDtypeStruct((rows, columns), jnp.bfloat16),
        in_specs=[vmem] * 5,
        out_specs=vmem,
        scratch_shapes=[
            pltpu.VMEM((n * rows, columns // n), jnp.bfloat16),
            pltpu.VMEM((n * rows, columns // n), jnp.bfloat16),
            pltpu.VMEM((rows, columns), jnp.bfloat16),
            pltpu.VMEM((rows, columns), jnp.float32),
            pltpu.VMEM((rows, columns), jnp.bfloat16),
            pltpu.VMEM((rows, states * LANES), jnp.bfloat16),
            pltpu.VMEM((rows, states * LANES), jnp.bfloat16),
            pltpu.VMEM((3, 8, x_dev * s_dev), jnp.float32),
            dma((chunks, n - 1)),
            dma((chunks, n - 1)),
            dma((chunks, n - 1)),
            dma((chunks, n - 1)),
            dma((4 + 2 * states,)),
            dma((4 + 2 * states,)),
        ],
        compiler_params=pltpu.CompilerParams(
            collective_id=0, has_side_effects=True, vmem_limit_bytes=60 * 1024 * 1024
        ),
        name="passage",
    )(
        adjoint_in.reshape(rows, columns),
        coef,
        scale,
        jnp.asarray(np.ascontiguousarray(table.T)),
        jnp.asarray(table),
    )
    return out.reshape(adjoint_in.shape)


def solution(mesh):
    in_specs = (
        P("row", "group", "blk", "span"),
        P("group", "blk", "span"),
        P("group"),
        P("group"),
        P(),
        P(),
    )
    out_specs = P("row", "group", "blk", "span")
    return jax.shard_map(
        on_device, mesh=mesh, in_specs=in_specs, out_specs=out_specs, check_vma=False
    )
```

```python
import math

import jax
import jax.numpy as jnp
import numpy as np
from jax import lax
from jax.experimental import pallas as pl
from jax.experimental.pallas import tpu as pltpu
from jax.sharding import PartitionSpec as P

AZ = 1024
MODES = 256
LANES = 128
MESH = pl.DeviceIdType.MESH


def make_table(points, modes_count):
    point_idx = np.arange(points, dtype=np.int64)
    mode_order = np.arange(1, modes_count + 1, dtype=np.int64)
    phase_idx = point_idx[:, None] * mode_order[None, :] % points
    angles = phase_idx.astype(np.float32) * np.float32(2.0 * math.pi / points)
    return np.concatenate([np.cos(angles), np.sin(angles)], axis=1).astype(jnp.bfloat16)


def lanes_at(start, size):
    return pl.ds(pl.multiple_of(start, LANES), size)


def rows_at(start, size):
    return pl.ds(pl.multiple_of(start, 16), size)


def kernel(
    rotor_lag, stator_lag, rotor_harm, stator_harm, coef_ref, field_ref, analysis_hbm, table_hbm,
    out_ref,
    slabs, flat, gath, stage, ret, local, across, first_x, last_x, coef_got, lined, analysis, table,
    in_sem, out_sem, table_sem, fwd_send, fwd_recv, back_send, back_recv, coef_send, coef_recv, halo_send, halo_recv,
):
    n = lax.axis_size("row")
    me = lax.axis_index("row")
    blks = lax.axis_size("blk")
    blk = lax.axis_index("blk")
    span = lax.axis_index("span")
    states, rows, x_dev, _ = slabs.shape
    plane = x_dev * LANES
    share = plane // n
    modes = table.shape[1] // 2
    step = min(rows, 64)

    peers = [lax.rem(me + off, n) for off in range(1, n)]
    blk_next = lax.rem(blk + 1, blks)
    blk_prev = lax.rem(blk + blks - 1, blks)
    span_other = 1 - span
    own = rows_at(me * rows, rows)

    def load_slab(c):
        return pltpu.make_async_copy(field_ref.at[:, c], slabs.at[c], in_sem.at[c])

    def store_slab(c):
        return pltpu.make_async_copy(slabs.at[c], out_ref.at[:, c], out_sem.at[c])

    load_tables = [
        pltpu.make_async_copy(analysis_hbm, analysis, table_sem.at[0]),
        pltpu.make_async_copy(table_hbm, table, table_sem.at[1]),
    ]

    @pl.loop(0, states)
    def _(c):
        load_slab(c).start()

    for copy in load_tables:
        copy.start()

    barrier = pltpu.get_barrier_semaphore()
    for peer in peers:
        pl.semaphore_signal(barrier, inc=1, device_id={"row": peer}, device_id_type=MESH)
    pl.semaphore_signal(barrier, inc=1, device_id={"blk": blk_next}, device_id_type=MESH)
    pl.semaphore_signal(barrier, inc=1, device_id={"blk": blk_prev}, device_id_type=MESH)
    pl.semaphore_signal(barrier, inc=1, device_id={"span": span_other}, device_id_type=MESH)

    def remote(src, dst, send_sem, recv_sem, where):
        return pltpu.make_async_remote_copy(
            src_ref=src, dst_ref=dst, send_sem=send_sem, recv_sem=recv_sem, device_id=where, device_id_type=MESH
        )

    def forward(c, off, peer):
        return remote(
            flat.at[c, :, lanes_at(peer * share, share)], gath.at[c, own, :],
            fwd_send.at[c, off], fwd_recv.at[c, off], {"row": peer},
        )

    def backward(c, off, peer):
        return remote(
            stage.at[c, rows_at(peer * rows, rows), :], ret.at[c, :, lanes_at(me * share, share)],
            back_send.at[c, off], back_recv.at[c, off], {"row": peer},
        )

    def halos(c):
        return [
            remote(flat.at[c], across.at[c], halo_send.at[c, 0], halo_recv.at[c, 0], {"span": span_other}),
            remote(
                flat.at[c, :, pl.ds(0, LANES)], first_x.at[c], halo_send.at[c, 1], halo_recv.at[c, 1],
                {"blk": blk_prev},
            ),
            remote(
                flat.at[c, :, pl.ds(plane - LANES, LANES)], last_x.at[c], halo_send.at[c, 2], halo_recv.at[c, 2],
                {"blk": blk_next},
            ),
        ]

    coef_copies = [
        remote(coef_ref, coef_got.at[i], coef_send.at[i], coef_recv.at[i], where)
        for i, where in enumerate(({"span": span_other}, {"blk": blk_prev}, {"blk": blk_next}))
    ]

    def flatten(c):
        @pl.loop(0, rows // step)
        def _(rb):
            here = rows_at(rb * step, step)
            lined[...] = slabs[c, here].astype(jnp.float32).reshape(step * x_dev, LANES)
            for x in range(x_dev):
                flat[c, here, x * LANES : (x + 1) * LANES] = lined[pl.ds(x, step, stride=x_dev), :].astype(jnp.bfloat16)

    load_slab(0).wait()
    flatten(0)
    pl.semaphore_wait(barrier, n + 2)

    @pl.loop(0, states)
    def _(c):
        @pl.when(c > 0)
        def _():
            load_slab(c).wait()
            flatten(c)

        for off, peer in enumerate(peers):
            forward(c, off, peer).start()
        for copy in halos(c):
            copy.start()

    for copy in coef_copies:
        copy.start()

    rotor = jnp.zeros((1, modes), jnp.float32)
    for h in range(rotor_lag.shape[0]):
        rotor = jnp.where(rotor_harm[...] == h, rotor_lag[h], rotor)
    stator = jnp.zeros((1, modes), jnp.float32)
    for h in range(stator_lag.shape[0]):
        stator = jnp.where(stator_harm[...] == h, stator_lag[h], stator)
    angle = jnp.where(blk * 2 < blks, rotor, stator)
    cos_scale = jnp.transpose(jnp.broadcast_to(jnp.cos(angle), (8, modes)))[:, 0:1]
    sin_scale = jnp.transpose(jnp.broadcast_to(jnp.sin(angle), (8, modes)))[:, 0:1]

    for copy in load_tables:
        copy.wait()

    @pl.loop(0, states)
    def _(c):
        gath[c, own, :] = flat[c, :, lanes_at(me * share, share)]
        for off, peer in enumerate(peers):
            forward(c, off, peer).wait_recv()
        coeffs = jnp.dot(analysis[...], gath[c], preferred_element_type=jnp.float32)
        cos_part = coeffs[:modes]
        sin_part = coeffs[modes:]
        rotated = jnp.concatenate(
            [cos_scale * cos_part + sin_scale * sin_part, cos_scale * sin_part - sin_scale * cos_part], axis=0
        ).astype(jnp.bfloat16)
        synthesis = jnp.dot(table[...], rotated, preferred_element_type=jnp.float32)
        stage[c] = (synthesis * (2.0 / AZ)).astype(jnp.bfloat16)
        for off, peer in enumerate(peers):
            backward(c, off, peer).start()
        ret[c, :, lanes_at(me * share, share)] = stage[c, own, :]

    for copy in coef_copies:
        copy.wait_recv()

    lane = lax.broadcasted_iota(jnp.int32, (step, LANES), 1)
    has_next = blk < blks - 1
    has_prev = blk > 0

    @pl.loop(0, states)
    def _(c):
        for copy in halos(c):
            copy.wait_recv()

        @pl.loop(0, rows // step)
        def _(rb):
            here = rows_at(rb * step, step)

            def field_at(x):
                return flat[c, here, x * LANES : (x + 1) * LANES].astype(jnp.float32)

            def coef_at(k, x):
                return coef_ref[k, x : x + 1, :]

            before = coef_got[2, 2, x_dev - 1 : x_dev, :] * last_x[c, here, :].astype(jnp.float32)
            after = coef_got[1, 1, 0:1, :] * first_x[c, here, :].astype(jnp.float32)
            before = jnp.where(has_prev, before, 0.0)
            after = jnp.where(has_next, after, 0.0)
            now = field_at(0)
            prev_term = before
            for x in range(x_dev):
                cols = slice(x * LANES, (x + 1) * LANES)
                later = field_at(x + 1) if x + 1 < x_dev else None
                next_term = coef_at(1, x + 1) * later if later is not None else after
                other = across[c, here, cols].astype(jnp.float32)
                right_edge = jnp.where(span == 0, coef_got[0, 3, x : x + 1, :] * other, 0.0)
                left_edge = jnp.where(span == 1, coef_got[0, 4, x : x + 1, :] * other, 0.0)
                right = pltpu.roll(jnp.where(lane == 0, right_edge, coef_at(3, x) * now), LANES - 1, 1)
                left = pltpu.roll(jnp.where(lane == LANES - 1, left_edge, coef_at(4, x) * now), 1, 1)
                local[c, here, cols] = coef_at(0, x) * now + next_term + prev_term + right + left
                prev_term = coef_at(2, x) * now
                now = later

    @pl.loop(0, states)
    def _(c):
        for off, peer in enumerate(peers):
            backward(c, off, peer).wait_recv()

        @pl.loop(0, rows // step)
        def _(rb):
            here = rows_at(rb * step, step)
            for x in range(x_dev):
                cols = slice(x * LANES, (x + 1) * LANES)
                lined[pl.ds(x, step, stride=x_dev), :] = local[c, here, cols] + ret[c, here, cols].astype(jnp.float32)
            slabs[c, here] = lined[...].reshape(step, x_dev, LANES).astype(jnp.bfloat16)

        store_slab(c).start()

    @pl.loop(0, states)
    def _(c):
        for off, peer in enumerate(peers):
            forward(c, off, peer).wait_send()
            backward(c, off, peer).wait_send()
        for copy in halos(c):
            copy.wait_send()
        store_slab(c).wait()

    for copy in coef_copies:
        copy.wait_send()


def on_device(adjoint_in, stencil_coef, rotor_lag, stator_lag, rotor_harm, stator_harm):
    rows, states, x_dev, s_dev = adjoint_in.shape
    n = lax.axis_size("row")
    table = make_table(AZ, MODES)
    vmem = pl.BlockSpec(memory_space=pltpu.VMEM)
    smem = pl.BlockSpec(memory_space=pltpu.SMEM)
    hbm = pl.BlockSpec(memory_space=pl.ANY)
    dma = pltpu.SemaphoreType.DMA
    share = x_dev * s_dev // n
    field16 = lambda shape: pltpu.VMEM(shape, jnp.bfloat16)
    field32 = lambda shape: pltpu.VMEM(shape, jnp.float32)
    return pl.pallas_call(
        kernel,
        out_shape=jax.ShapeDtypeStruct(adjoint_in.shape, jnp.bfloat16),
        in_specs=[smem, smem, vmem, vmem, vmem, hbm, hbm, hbm],
        out_specs=hbm,
        scratch_shapes=[
            field16((states, rows, x_dev, s_dev)),
            field16((states, rows, x_dev * s_dev)),
            field16((states, n * rows, share)),
            field16((states, n * rows, share)),
            field16((states, rows, x_dev * s_dev)),
            field32((states, rows, x_dev * s_dev)),
            field16((states, rows, x_dev * s_dev)),
            field16((states, rows, s_dev)),
            field16((states, rows, s_dev)),
            field32((3, 5, x_dev, s_dev)),
            field32((min(rows, 64) * x_dev, s_dev)),
            field16((2 * MODES, AZ)),
            field16((AZ, 2 * MODES)),
            dma((states,)),
            dma((states,)),
            dma((2,)),
            dma((states, n - 1)),
            dma((states, n - 1)),
            dma((states, n - 1)),
            dma((states, n - 1)),
            dma((3,)),
            dma((3,)),
            dma((states, 3)),
            dma((states, 3)),
        ],
        compiler_params=pltpu.CompilerParams(
            collective_id=0, has_side_effects=True, vmem_limit_bytes=60 * 1024 * 1024
        ),
        name="passage",
    )(
        rotor_lag,
        stator_lag,
        rotor_harm.reshape(1, MODES),
        stator_harm.reshape(1, MODES),
        stencil_coef,
        adjoint_in,
        jnp.asarray(np.ascontiguousarray(table.T)),
        jnp.asarray(table),
    )


def solution(mesh):
    in_specs = (
        P("row", "group", "blk", "span"),
        P("group", "blk", "span"),
        P("group"),
        P("group"),
        P(),
        P(),
    )
    out_specs = P("row", "group", "blk", "span")
    return jax.shard_map(
        on_device, mesh=mesh, in_specs=in_specs, out_specs=out_specs, check_vma=False
    )
```
